256 devices in a mesh: region: 8 (over x, z_hi), leaf: 32 (over z_lo, y, core).
Axes of the slice: x: 4, y: 4, z: 8 (z_hi: 2, z_lo: 4; z = z_hi * 4 + z_lo), core: 2. Of those that a mesh axis runs over, the one named last changes fastest.
Arguments:
- whiten: bfloat16 [256, 1024, 1024], P(('region', 'leaf')), as said below
- leaf_root: bfloat16 [256, 1024, 512], P(('region', 'leaf')), may hold values from -6 to 6
- leaf_region: bfloat16 [256, 1024, 512], P(('region', 'leaf')), may hold values from -6 to 6
- root_factor: bfloat16 [512, 512], P('region'), may hold values from -0.25 to 0.25
- root_adjoint: bfloat16 [512, 512], P('region'), may hold values from -0.25 to 0.25
- region_factor: bfloat16 [8, 512, 512], P('region', 'leaf'), may hold values from -0.25 to 0.25
- region_adjoint: bfloat16 [8, 512, 512], P('region', 'leaf'), may hold values from -0.25 to 0.25
Outputs:
- grad_root_basis: bfloat16 [256, 1024, 512], P(('region', 'leaf'))
- grad_region_basis: bfloat16 [256, 1024, 512], P(('region', 'leaf'))
- grad_root_factor: float32 [512, 512], P('leaf')
- grad_region_factor: float32 [8, 512, 512], P('region', 'leaf')
The draws below stay inside these ranges and needn't reach their ends.
Inputs may be any that keep to these rules, and one draw needn't show every extreme that they name: `whiten`: each whitening matrix is lower triangular with a positive diagonal.
All inputs are finite; a program needn't handle non-finite values.
Results may differ from the reference program's by a relative error of at most 0.018.
Values may be sent and summed in bfloat16 or wider, within the bound.
No kernel may reach another device: no remote copies, remote signals or barrier semaphores. Data moves between devices by JAX's collectives and lax.ppermute only.
A program may use at most 64 MiB of HBM per device.

```python
import jax
import jax.numpy as jnp
from jax import lax

R = 512
M = 512
OBS = 1024
LEAVES = 256
REGIONS = 8


def draw_whiten(key, part):
    first, second = jax.random.split(jax.random.fold_in(key, 17))
    spread = 0.5 * jax.random.normal(first, (LEAVES, OBS, OBS), jnp.float32) / jnp.sqrt(OBS * 1.0)
    lower = jnp.tril(spread, -1)
    diag_vals = jnp.exp(jax.random.uniform(second, (LEAVES, OBS), jnp.float32, jnp.log(0.5), jnp.log(2.0)))
    eye_mat = jnp.eye(OBS, dtype=jnp.float32)
    return (lower + diag_vals[:, :, None] * eye_mat[None]).astype(jnp.bfloat16)


def block_levels(key, extent, shards, least, high):
    level, own = 1.0, jax.random.fold_in(key, 6)
    for position, blocks in shards:
        heights = jnp.exp(jax.random.uniform(jax.random.fold_in(own, position), (blocks,), jnp.float32, least / len(shards), high / len(shards)))
        level = level * jnp.repeat(heights, extent[position] // blocks).reshape([-1 if axis == position else 1 for axis in range(len(extent))])
    return level


def centred(own_key, extent, deviation, bound, cuts=(), held_as=jnp.bfloat16):
    array = deviation * jax.random.normal(own_key, extent, jnp.float32)
    if cuts:
        array = array * block_levels(own_key, extent, cuts, -0.22, 0.18)
    return jnp.clip(array, -bound, bound).astype(held_as)


def setup_inputs(seed: int = 0) -> dict:
    keys = jax.random.split(jax.random.key(seed), 8)
    return {
        "whiten": draw_whiten(jax.random.fold_in(keys[7], 71), 0),
        "leaf_root": centred(keys[1], (LEAVES, OBS, R), 1.0, 6.0, ((0, 256),)),
        "leaf_region": centred(keys[2], (LEAVES, OBS, M), 1.0, 6.0, ((0, 256),)),
        "root_factor": centred(keys[3], (R, R), R ** -0.5, 0.25, ((0, 8),)),
        "root_adjoint": centred(keys[4], (R, R), R ** -0.5, 0.25, ((0, 8),)),
        "region_factor": centred(keys[5], (REGIONS, M, M), M ** -0.5, 0.25, ((0, 8), (1, 32))),
        "region_adjoint": centred(keys[6], (REGIONS, M, M), M ** -0.5, 0.25, ((0, 8), (1, 32))),
    }


def matmul(left, right):
    return jnp.dot(left.astype(jnp.float32), right.astype(jnp.float32), preferred_element_type=jnp.float32)


def reference(whiten, leaf_root, leaf_region, root_factor, root_adjoint, region_factor, region_adjoint):
    root_wide = root_adjoint.astype(jnp.float32)
    region_wide = region_adjoint.astype(jnp.float32)
    root_sym = (root_wide + root_wide.T).astype(jnp.bfloat16)
    region_sym = (region_wide + jnp.swapaxes(region_wide, 1, 2)).astype(jnp.bfloat16)
    per_region = LEAVES // REGIONS

    def visit(carry, inputs):
        root_total, region_total = carry
        factor_inv, base_root, base_region, number = inputs
        owner = (number // per_region).astype(jnp.int32)
        own_factor = lax.dynamic_index_in_dim(region_factor, owner, 0, keepdims=False)
        own_sym = lax.dynamic_index_in_dim(region_sym, owner, 0, keepdims=False)
        root_basis = matmul(base_root, root_factor).astype(jnp.bfloat16)
        region_basis = matmul(base_region, own_factor).astype(jnp.bfloat16)
        root_white = matmul(factor_inv, root_basis).astype(jnp.bfloat16)
        region_white = matmul(factor_inv, region_basis).astype(jnp.bfloat16)
        root_dwhite = matmul(root_white, root_sym).astype(jnp.bfloat16)
        region_dwhite = matmul(region_white, own_sym).astype(jnp.bfloat16)
        grad_root = matmul(factor_inv.T, root_dwhite).astype(jnp.bfloat16)
        grad_region = matmul(factor_inv.T, region_dwhite).astype(jnp.bfloat16)
        root_total = root_total + matmul(base_root.T, grad_root) / OBS
        region_term = matmul(base_region.T, grad_region) / OBS
        old = lax.dynamic_index_in_dim(region_total, owner, 0, keepdims=True)
        region_total = lax.dynamic_update_index_in_dim(region_total, old + region_term[None], owner, 0)
        return (root_total, region_total), (grad_root, grad_region)

    start = (jnp.zeros((R, R), jnp.float32), jnp.zeros((REGIONS, M, M), jnp.float32))
    numbers = jnp.arange(LEAVES, dtype=jnp.int32)
    (root_total, region_total), (grad_root_basis, grad_region_basis) = lax.scan(
        visit, start, (whiten, leaf_root, leaf_region, numbers))
    return grad_root_basis, grad_region_basis, root_total, region_total
```

```python
import functools

import jax
import jax.numpy as jnp
from jax import lax
from jax.experimental import pallas as pl
from jax.experimental.pallas import tpu as pltpu
from jax.sharding import PartitionSpec as P

BF = jnp.bfloat16
F32 = jnp.float32
BOTH = ("region", "leaf")
Z_LO, Y, CORE, X, Z_HI = 4, 4, 2, 4, 2
LEAF = Z_LO * Y * CORE
TILE = 256


def place(x, y, z, c):
    return (x * Z_HI + z // Z_LO) * LEAF + (z % Z_LO) * Y * CORE + y * CORE + c


def coordinates(i):
    r, leaf = divmod(i, LEAF)
    x, hi = divmod(r, Z_HI)
    lo, rest = divmod(leaf, Y * CORE)
    y, c = divmod(rest, CORE)
    return x, y, hi * Z_LO + lo, c


def pairs(move):
    return [(i, place(*move(*coordinates(i)))) for i in range(X * Z_HI * LEAF)]


SWAP_CORES = pairs(lambda x, y, z, c: (x, y, z, 1 - c))
MIRROR_Z = pairs(lambda x, y, z, c: (x, y, 7 - z, c))
ALONG_Y = [[place(0, y, lo, c) for y in range(Y)] for lo in range(Z_LO) for c in range(CORE)]
ALONG_Z_LO = [[place(0, y, lo, c) for lo in range(Z_LO)] for y in range(Y) for c in range(CORE)]
ALONG_Z = [
    [place(x, y, z, c) for z in range(Z_LO * Z_HI)]
    for x in range(X)
    for y in range(Y)
    for c in range(CORE)
]
ALONG_X = [[x * Z_HI + hi for x in range(X)] for hi in range(Z_HI)]


def exchange(pieces, axis, groups):
    return lax.all_to_all(pieces, axis, 0, 0, tiled=True, axis_index_groups=groups)


def to_each(x, axis, groups):
    return exchange(jnp.broadcast_to(x[None], (len(groups[0]), *x.shape)), axis, groups)


def added(pieces):
    return pieces.astype(F32).sum(axis=0)


def dot(a, b, dims=((1,), (0,))):
    return lax.dot_general(a, b, (dims, ((), ())), preferred_element_type=F32)


def call(kernel, out_shape, flops, n_scalars, *args):
    operands = args
    moved = sum(a.size * a.dtype.itemsize for a in operands) + sum(
        int(functools.reduce(lambda p, q: p * q, s.shape, 1)) * s.dtype.itemsize for s in out_shape
    )
    specs = [pl.BlockSpec(memory_space=pltpu.SMEM)] * n_scalars + [
        pl.BlockSpec(memory_space=pltpu.VMEM)
    ] * (len(args) - n_scalars)
    return pl.pallas_call(
        kernel,
        out_shape=out_shape,
        in_specs=specs,
        out_specs=[pl.BlockSpec(memory_space=pltpu.VMEM)] * len(out_shape),
        compiler_params=pltpu.CompilerParams(vmem_limit_bytes=48 * 1024 * 1024),
        cost_estimate=pl.CostEstimate(flops=flops, bytes_accessed=moved, transcendentals=0),
    )(*args)


def gram_kernel(core_ref, w_ref, root_ref, region_ref, white_ref, own_ref, send_ref):
    n = w_ref.shape[0]
    width = root_ref.shape[1]
    core = core_ref[0]
    for i in range(n // TILE):
        rows = slice(TILE * i, TILE * (i + 1))
        k = TILE * (i + 1)
        w = w_ref[rows, :k]
        white_ref[rows, :width] = dot(w, root_ref[:k, :]).astype(BF)
        white_ref[rows, width:] = dot(w, region_ref[:k, :]).astype(BF)
    for level in range(2):
        cols = slice(level * width, (level + 1) * width)
        a = white_ref[:, cols]
        for i in range(width // TILE):
            g = dot(a[:, TILE * i : TILE * (i + 1)], a, ((0,), (0,)))
            g = g.reshape(TILE // 32, 2, 16, width)
            rows = slice(TILE // 2 * i, TILE // 2 * (i + 1))
            own = jnp.where(core == 0, g[:, 0], g[:, 1])
            send = jnp.where(core == 0, g[:, 1], g[:, 0])
            own_ref[level, rows, :] = own.reshape(TILE // 2, width).astype(BF)
            send_ref[level, rows, :] = send.reshape(TILE // 2, width).astype(BF)


def back_kernel(w_ref, white_ref, out_ref):
    n = w_ref.shape[0]
    width = white_ref.shape[1] // 2
    for j in range(n // TILE):
        rows = slice(TILE * j, TILE * (j + 1))
        w = w_ref[TILE * j :, rows]
        for level in range(2):
            cols = slice(level * width, (level + 1) * width)
            out_ref[rows, cols] = dot(w, white_ref[TILE * j :, cols], ((0,), (0,))).astype(BF)


def factor_kernel(core_ref, root_mine, root_came, region_mine, region_came, root_out, region_out):
    first = core_ref[0] == 0
    mine, came = root_mine[...], root_came[...]
    factor = jnp.where(first, mine, came)
    adjoint = jnp.where(first, came, mine)
    root_out[...] = (dot(factor, adjoint) + dot(factor, adjoint, ((1,), (1,)))).astype(BF)

    def merged(part):
        a, b = region_mine[part], region_came[part]
        low = jnp.where(first, a, b)
        high = jnp.where(first, b, a)
        return jnp.stack([low, high], axis=1).reshape(512, 512)

    factor, adjoint = merged(0), merged(1)
    region_out[...] = (dot(factor, adjoint) + dot(factor, adjoint, ((1,), (1,)))).astype(BF)


def grads_kernel(back_ref, root_ref, region_ref, root_out, region_out):
    width = root_ref.shape[0]
    for i in range(back_ref.shape[0] // TILE):
        rows = slice(TILE * i, TILE * (i + 1))
        root_out[0, rows, :] = dot(back_ref[rows, :width], root_ref[...]).astype(BF)
        region_out[0, rows, :] = dot(back_ref[rows, width:], region_ref[...]).astype(BF)


def rows_kernel(scale, pieces_ref, factor_ref, out_ref):
    total = pieces_ref[0].astype(F32)
    for k in range(1, pieces_ref.shape[0]):
        total = total + pieces_ref[k].astype(F32)
    high = total.astype(BF)
    low = (total - high.astype(F32)).astype(BF)
    out_ref[...] = (dot(high, factor_ref[...]) + dot(low, factor_ref[...])) * scale


def shaped(*shape, dtype=BF):
    return jax.ShapeDtypeStruct(shape, dtype)


def on_device(
    whiten, leaf_root, leaf_region, root_factor, root_adjoint, region_factor, region_adjoint
):
    obs, width = leaf_root.shape[1:]
    core = lax.axis_index("leaf") % CORE
    hi = lax.axis_index("region") % Z_HI
    cores = core.astype(jnp.int32).reshape(1)
    w = whiten[0]

    root_mine = jnp.where(core == 0, root_factor, root_adjoint)
    root_other = lax.ppermute(root_mine, BOTH, MIRROR_Z)
    root_two = jnp.where(
        hi == 0, jnp.stack([root_mine, root_other]), jnp.stack([root_other, root_mine])
    )
    root_mine = to_each(root_two, "region", ALONG_X).reshape(width, width)
    root_came = lax.ppermute(root_mine, BOTH, SWAP_CORES)

    region_mine = jnp.stack([region_factor[0], region_adjoint[0]])
    region_mine = to_each(region_mine, "leaf", ALONG_Z_LO)
    region_mine = to_each(region_mine, "leaf", ALONG_Y)
    region_mine = jnp.transpose(region_mine, (2, 1, 0, 3, 4)).reshape(2, Z_LO * Y, 16, width)
    region_came = lax.ppermute(region_mine, BOTH, SWAP_CORES)

    white, own, send = call(
        gram_kernel,
        [shaped(obs, 2 * width), shaped(2, width // 2, width), shaped(2, width // 2, width)],
        2 * 2 * (obs * obs * width + obs * width * width),
        1,
        cores,
        w,
        leaf_root[0],
        leaf_region[0],
    )
    came = lax.ppermute(send, BOTH, SWAP_CORES)
    total = (own.astype(F32) + came.astype(F32)).astype(BF)
    total = total.reshape(2, Z_LO, Y, 16, width).transpose(2, 0, 1, 3, 4)
    total = added(exchange(total, "leaf", ALONG_Y)).astype(BF)
    root_pieces = exchange(jnp.concatenate([total[0], total[0]]), BOTH, ALONG_Z)
    region_pieces = exchange(total[1], "leaf", ALONG_Z_LO)
    root_rows = added(root_pieces).astype(BF)
    root_pieces = to_each(root_rows, "region", ALONG_X)

    (back,) = call(
        back_kernel, [shaped(obs, 2 * width)], 2 * 2 * obs * obs * width, 0, w, white
    )
    root_product, region_product = call(
        factor_kernel,
        [shaped(width, width)] * 2,
        2 * 4 * width**3,
        1,
        cores,
        root_mine,
        root_came,
        region_mine,
        region_came,
    )
    grad_root, grad_region = call(
        grads_kernel,
        [shaped(1, obs, width)] * 2,
        2 * 2 * obs * width * width,
        0,
        back,
        root_product,
        region_product,
    )
    rows = functools.partial(rows_kernel, 1.0 / obs)
    out = shaped(16, width, dtype=F32)
    (region_part,) = call(
        rows, [out], 4 * 16 * width * width, 0, region_pieces, region_product
    )
    (root_part,) = call(rows, [out], 4 * 16 * width * width, 0, root_pieces, root_product)
    return grad_root, grad_region, root_part, region_part[None]


def solution(mesh):
    return jax.shard_map(
        on_device,
        mesh=mesh,
        in_specs=(
            P(("region", "leaf"), None, None),
            P(("region", "leaf"), None, None),
            P(("region", "leaf"), None, None),
            P("region", None),
            P("region", None),
            P("region", "leaf", None),
            P("region", "leaf", None),
        ),
        out_specs=(
            P(("region", "leaf"), None, None),
            P(("region", "leaf"), None, None),
            P("leaf", None),
            P("region", "leaf", None),
        ),
        check_vma=False,
    )
```

```python
import functools
import math

import jax
import jax.numpy as jnp
from jax import lax
from jax.experimental import pallas as pl
from jax.experimental.pallas import tpu as pltpu
from jax.sharding import PartitionSpec as P

BF = jnp.bfloat16
F32 = jnp.float32
BOTH = ("region", "leaf")
Z_LO, Y, CORE, X, Z_HI = 4, 4, 2, 4, 2
LEAF = Z_LO * Y * CORE
TILE = 256


def place(x, y, z, c):
    return (x * Z_HI + z // Z_LO) * LEAF + (z % Z_LO) * Y * CORE + y * CORE + c


def coordinates(i):
    r, leaf = divmod(i, LEAF)
    x, hi = divmod(r, Z_HI)
    lo, rest = divmod(leaf, Y * CORE)
    y, c = divmod(rest, CORE)
    return x, y, hi * Z_LO + lo, c


def pairs(move):
    return [(i, place(*move(*coordinates(i)))) for i in range(X * Z_HI * LEAF)]


SWAP_CORES = pairs(lambda x, y, z, c: (x, y, z, 1 - c))
MIRROR_Z = pairs(lambda x, y, z, c: (x, y, 7 - z, c))
Z_ONE = pairs(lambda x, y, z, c: (x, y, z ^ 1, c))
Z_TWO = pairs(lambda x, y, z, c: (x, y, z ^ 2, c))
Y_ONE = pairs(lambda x, y, z, c: (x, y ^ 1, z, c))
Y_THREE = pairs(lambda x, y, z, c: (x, y ^ 3, z, c))
X_ONE = pairs(lambda x, y, z, c: (x ^ 1, y, z, c))
X_TWO = pairs(lambda x, y, z, c: (x ^ 2, y, z, c))
X_THREE = pairs(lambda x, y, z, c: (x ^ 3, y, z, c))
ALONG_Y = [[place(0, y, lo, c) for y in range(Y)] for lo in range(Z_LO) for c in range(CORE)]
ALONG_Z = [
    [place(x, y, z, c) for z in range(Z_LO * Z_HI)]
    for x in range(X)
    for y in range(Y)
    for c in range(CORE)
]


def exchange(pieces, axis, groups):
    return lax.all_to_all(pieces, axis, 0, 0, tiled=True, axis_index_groups=groups)


def sent(x, moves):
    return lax.ppermute(x, BOTH, moves)


def after(x, *others):
    return lax.optimization_barrier((x, *others))[0]


def doubled(x, moves):
    return jnp.stack([x, sent(x, moves)])


def added(pieces):
    return pieces.astype(F32).sum(axis=0)


def dot(a, b, dims=((1,), (0,))):
    return lax.dot_general(a, b, (dims, ((), ())), preferred_element_type=F32)


VMEM, SMEM, HBM = pltpu.VMEM, pltpu.SMEM, pltpu.HBM


def call(kernel, ins, outs, scratch, flops, mib, *args):
    moved = 2 * sum(a.size for a in args) + 2 * sum(math.prod(s.shape) for s, _ in outs)
    args = [pltpu.with_memory_space_constraint(a, m) for a, m in zip(args, ins)]
    return pl.pallas_call(
        kernel,
        out_shape=[s if s.dtype == F32 else m(s.shape, s.dtype) for s, m in outs],
        in_specs=[pl.BlockSpec(memory_space=m) for m in ins],
        out_specs=[pl.BlockSpec(memory_space=m) for _, m in outs],
        scratch_shapes=scratch,
        compiler_params=pltpu.CompilerParams(vmem_limit_bytes=mib * 1024 * 1024),
        cost_estimate=pl.CostEstimate(flops=flops, bytes_accessed=moved, transcendentals=0),
    )(*args)


def position():
    r, leaf = lax.axis_index("region"), lax.axis_index("leaf")
    x, hi = lax.div(r, Z_HI), lax.rem(r, Z_HI)
    lo, rest = lax.div(leaf, Y * CORE), lax.rem(leaf, Y * CORE)
    return x, lax.div(rest, CORE), hi, lo, lax.rem(rest, CORE)


def shaped(*shape, dtype=BF):
    return jax.ShapeDtypeStruct(shape, dtype)


def dma(n):
    return pltpu.SemaphoreType.DMA((n,))


def prepare_kernel(root_f, root_a, region_f, region_a, root_out, region_out, sem):
    core = position()[4]
    copies = [
        pltpu.make_async_copy(region_f.at[0], region_out.at[0], sem.at[0]),
        pltpu.make_async_copy(region_a.at[0], region_out.at[1], sem.at[1]),
    ]
    for copy in copies:
        copy.start()

    @pl.when(core == 0)
    def _():
        copy = pltpu.make_async_copy(root_f, root_out, sem.at[2])
        copy.start()
        copy.wait()

    @pl.when(core != 0)
    def _():
        copy = pltpu.make_async_copy(root_a, root_out, sem.at[2])
        copy.start()
        copy.wait()

    for copy in copies:
        copy.wait()


def gram_kernel(
    w_hbm, root_hbm, region_hbm, white_hbm, own_ref, send_ref, w, leaf, white, in_sem, out_sem
):
    n, width = root_hbm.shape
    tiles = n // TILE
    first = position()[4] == 0
    arrivals, leaving = [], []
    for i in range(tiles):
        rows, k = pl.ds(TILE * i, TILE), pl.ds(0, TILE * (i + 1))
        arrivals.append(
            [
                pltpu.make_async_copy(w_hbm.at[rows, k], w.at[rows, k], in_sem.at[3 * i]),
                pltpu.make_async_copy(
                    root_hbm.at[rows], leaf.at[rows, pl.ds(0, width)], in_sem.at[3 * i + 1]
                ),
                pltpu.make_async_copy(
                    region_hbm.at[rows], leaf.at[rows, pl.ds(width, width)], in_sem.at[3 * i + 2]
                ),
            ]
        )
        for copy in arrivals[-1]:
            copy.start()
    for i in range(tiles):
        for copy in arrivals[i]:
            copy.wait()
        rows, k = slice(TILE * i, TILE * (i + 1)), TILE * (i + 1)
        for level in range(2):
            cols = slice(level * width, (level + 1) * width)
            white[rows, cols] = dot(w[rows, :k], leaf[:k, cols]).astype(BF)
        rows = pl.ds(TILE * i, TILE)
        leaving.append(
            pltpu.make_async_copy(white.at[rows], white_hbm.at[rows], out_sem.at[i])
        )
        leaving[-1].start()
    for level in range(2):
        a = white[:, level * width : (level + 1) * width]
        for i in range(width // TILE):
            g = dot(a[:, TILE * i : TILE * (i + 1)], a, ((0,), (0,)))
            g = g.reshape(TILE // 32, 2, 16, width)
            for b in range(TILE // 32):
                lo, y = divmod(i * (TILE // 32) + b, Y)
                own_ref[y, level, lo] = jnp.where(first, g[b, 0], g[b, 1]).astype(BF)
                send_ref[y, level, lo] = jnp.where(first, g[b, 1], g[b, 0]).astype(BF)
    for copy in leaving:
        copy.wait()


def back_kernel(w_hbm, white_hbm, out_hbm, w, white, out, in_sem, out_sem):
    n = w_hbm.shape[0]
    width = white.shape[1] // 2
    tiles = n // TILE
    arrivals, leaving = [], []
    for i in reversed(range(tiles)):
        rows, k = pl.ds(TILE * i, TILE), pl.ds(0, TILE * (i + 1))
        pair = [
            pltpu.make_async_copy(w_hbm.at[rows, k], w.at[rows, k], in_sem.at[2 * i]),
            pltpu.make_async_copy(white_hbm.at[rows], white.at[rows], in_sem.at[2 * i + 1]),
        ]
        for copy in pair:
            copy.start()
        arrivals.append(pair)
    for i, pair in zip(reversed(range(tiles)), arrivals):
        for copy in pair:
            copy.wait()
        rows = slice(TILE * i, TILE * (i + 1))
        for level in range(2):
            cols = slice(level * width, (level + 1) * width)
            out[rows, cols] = dot(
                w[TILE * i :, rows], white[TILE * i :, cols], ((0,), (0,))
            ).astype(BF)
        rows = pl.ds(TILE * i, TILE)
        leaving.append(pltpu.make_async_copy(out.at[rows], out_hbm.at[rows], out_sem.at[i]))
        leaving[-1].start()
    for copy in leaving:
        copy.wait()


def merge_kernel(own, came, out):
    for k in range(own.shape[0]):
        out[k] = (own[k].astype(F32) + came[k].astype(F32)).astype(BF)


def sum_kernel(pieces, out):
    for level in range(2):
        for lo in range(Z_LO):
            total = pieces[0, level, lo].astype(F32)
            for k in range(1, Y):
                total = total + pieces[k, level, lo].astype(F32)
            total = total.astype(BF)
            for hi in range(Z_HI):
                out[hi * Z_LO + lo, level] = total


def product_of_rows(total, factor, scale):
    high = total.astype(BF)
    low = (total - high.astype(F32)).astype(BF)
    out = dot(jnp.concatenate([high, low]), factor)
    return (out[:16] + out[16:]) * scale


def finish_kernel(
    scale,
    root_mine,
    root_came,
    region_mine,
    region_came,
    pieces,
    back_hbm,
    root_hbm,
    region_hbm,
    rows_out,
    root_product,
    f,
    a,
    region_product,
    back,
    root,
    region,
    in_sem,
    out_sem,
):
    x, y, hi, lo, core = position()
    first = core == 0
    n, width = back.shape[0], f.shape[0]
    arrivals, leaving = [], []
    for i in range(n // TILE):
        rows = pl.ds(TILE * i, TILE)
        arrivals.append(pltpu.make_async_copy(back_hbm.at[rows], back.at[rows], in_sem.at[i]))
        arrivals[-1].start()

    def leave(part, out, i, level):
        rows = pl.ds(TILE * i, TILE)
        copy = pltpu.make_async_copy(
            part.at[rows], out.at[0, rows], out_sem.at[2 * i + level]
        )
        copy.start()
        leaving.append(copy)

    for j in range(X * Z_HI):
        rows = slice(64 * j, 64 * (j + 1))
        v = x ^ (j // Z_HI)
        t = v >> 1
        slot = t * 4 + ((v & 1) ^ t) * 2 + (hi ^ (j % Z_HI))
        mine, came = root_mine[slot], root_came[slot]
        f[rows, :] = jnp.where(first, mine, came)
        a[rows, :] = jnp.where(first, came, mine)
    product = dot(f[...], a[...]) + dot(f[...], a[...], ((1,), (1,)))
    root_product[...] = product.astype(BF)
    for i in range(n // TILE):
        arrivals[i].wait()
        rows = slice(TILE * i, TILE * (i + 1))
        root[rows, :] = dot(back[rows, :width], root_product[...]).astype(BF)
        leave(root, root_hbm, i, 0)
    for j in range(Z_LO * Y):
        v = y ^ (j % Y)
        t = v >> 1
        slot = t * 8 + ((v & 1) ^ t) * 4 + (lo ^ (j // Y))
        for part, out in ((0, f), (1, a)):
            mine, came = region_mine[slot, part], region_came[slot, part]
            out[32 * j : 32 * j + 16, :] = jnp.where(first, mine, came)
            out[32 * j + 16 : 32 * j + 32, :] = jnp.where(first, came, mine)
    product = dot(f[...], a[...]) + dot(f[...], a[...], ((1,), (1,)))
    region_product[...] = product.astype(BF)
    for i in range(n // TILE):
        rows = slice(TILE * i, TILE * (i + 1))
        region[rows, :] = dot(back[rows, width:], region_product[...]).astype(BF)
        leave(region, region_hbm, i, 1)
    total = pieces[hi * Z_LO, 1].astype(F32)
    for k in range(1, Z_LO):
        total = total + pieces[hi * Z_LO + k, 1].astype(F32)
    rows_out[0] = product_of_rows(total, region_product[...], scale)
    for copy in leaving:
        copy.wait()


def root_rows_kernel(scale, a, b, c, d, factor, out_ref):
    total = (a[...].astype(F32) + b[...].astype(F32)) + (c[...].astype(F32) + d[...].astype(F32))
    out_ref[...] = product_of_rows(total, factor[...], scale)


def on_device(
    whiten, leaf_root, leaf_region, root_factor, root_adjoint, region_factor, region_adjoint
):
    obs, width = leaf_root.shape[1:]
    tiles = obs // TILE
    w = whiten[0]

    root_mine, region_mine = call(
        prepare_kernel,
        [HBM] * 4,
        [(shaped(64, width), VMEM), (shaped(2, 16, width), VMEM)],
        [dma(3)],
        0,
        4,
        root_factor,
        root_adjoint,
        region_factor,
        region_adjoint,
    )
    w_first = after(w, root_mine)
    root_mine = doubled(root_mine, MIRROR_Z)
    region_mine = doubled(region_mine, Z_ONE)

    square, strip = VMEM((obs, 2 * width), BF), VMEM((obs, width), BF)
    half = shaped(Y, 2, Z_LO, 16, width)
    white, own, send = call(
        gram_kernel,
        [HBM] * 3,
        [(shaped(obs, 2 * width), HBM), (half, VMEM), (half, VMEM)],
        [VMEM((obs, obs), BF), square, square, dma(3 * tiles), dma(tiles)],
        2 * 2 * (obs * obs * width + obs * width * width),
        20,
        w_first,
        leaf_root[0],
        leaf_region[0],
    )
    send = after(send, region_mine, root_mine)
    region_mine = doubled(after(region_mine, send), Z_TWO)
    root_mine = doubled(after(root_mine, send), X_ONE)
    (total,) = call(
        merge_kernel, [VMEM] * 2, [(half, VMEM)], [], 0, 8, own, sent(send, SWAP_CORES)
    )
    (back,) = call(
        back_kernel,
        [HBM] * 2,
        [(shaped(obs, 2 * width), HBM)],
        [VMEM((obs, obs), BF), square, square, dma(2 * tiles), dma(tiles)],
        2 * 2 * obs * obs * width,
        20,
        w,
        after(white, total),
    )
    region_mine = doubled(after(region_mine, back), Y_ONE)
    root_mine = doubled(after(root_mine, back), X_THREE)
    root_mine = root_mine.reshape(X * Z_HI, 64, width)
    (total,) = call(
        sum_kernel,
        [VMEM],
        [(shaped(Z_LO * Z_HI, 2, 16, width), VMEM)],
        [],
        0,
        8,
        exchange(total, "leaf", ALONG_Y),
    )
    region_mine = doubled(after(region_mine, total), Y_THREE)
    region_mine = region_mine.reshape(Y * Z_LO, 2, 16, width)
    root_came = sent(after(root_mine, total), SWAP_CORES)
    pieces = exchange(total, BOTH, ALONG_Z)
    root_rows = added(pieces[:, 0]).astype(BF)
    region_came = sent(after(region_mine, root_rows), SWAP_CORES)
    others = [sent(root_rows, moves) for moves in (X_ONE, X_THREE, X_TWO)]

    scale = 1.0 / obs
    factor = VMEM((width, width), BF)
    grad_root, grad_region, region_part, root_product = call(
        functools.partial(finish_kernel, scale),
        [VMEM] * 5 + [HBM],
        [
            (shaped(1, obs, width), HBM),
            (shaped(1, obs, width), HBM),
            (shaped(1, 16, width, dtype=F32), VMEM),
            (shaped(width, width), VMEM),
        ],
        [factor, factor, factor, square, strip, strip, dma(tiles), dma(2 * tiles)],
        2 * 2 * obs * width * width + 8 * width**3,
        20,
        root_mine,
        root_came,
        region_mine,
        region_came,
        pieces,
        back,
    )
    (root_part,) = call(
        functools.partial(root_rows_kernel, scale),
        [VMEM] * 5,
        [(shaped(16, width, dtype=F32), VMEM)],
        [],
        4 * 16 * width * width,
        4,
        root_rows,
        *others,
        root_product,
    )
    return grad_root, grad_region, root_part, region_part


def solution(mesh):
    return jax.shard_map(
        on_device,
        mesh=mesh,
        in_specs=(
            P(("region", "leaf"), None, None),
            P(("region", "leaf"), None, None),
            P(("region", "leaf"), None, None),
            P("region", None),
            P("region", None),
            P("region", "leaf", None),
            P("region", "leaf", None),
        ),
        out_specs=(
            P(("region", "leaf"), None, None),
            P(("region", "leaf"), None, None),
            P("leaf", None),
            P("region", "leaf", None),
        ),
        check_vma=False,
    )
```

```python
import functools
import math

import jax
import jax.numpy as jnp
from jax import lax
from jax.experimental import pallas as pl
from jax.experimental.pallas import tpu as pltpu
from jax.sharding import PartitionSpec as P

BF = jnp.bfloat16
F32 = jnp.float32
BOTH = ("region", "leaf")
Z_LO, Y, CORE, X, Z_HI = 4, 4, 2, 4, 2
LEAF = Z_LO * Y * CORE
TILE = 256


def place(x, y, z, c):
    return (x * Z_HI + z // Z_LO) * LEAF + (z % Z_LO) * Y * CORE + y * CORE + c


def coordinates(i):
    r, leaf = divmod(i, LEAF)
    x, hi = divmod(r, Z_HI)
    lo, rest = divmod(leaf, Y * CORE)
    y, c = divmod(rest, CORE)
    return x, y, hi * Z_LO + lo, c


def pairs(move):
    return [(i, place(*move(*coordinates(i)))) for i in range(X * Z_HI * LEAF)]


SWAP_CORES = pairs(lambda x, y, z, c: (x, y, z, 1 - c))
MIRROR_Z = pairs(lambda x, y, z, c: (x, y, 7 - z, c))
Z_ONE = pairs(lambda x, y, z, c: (x, y, z ^ 1, c))
Z_TWO = pairs(lambda x, y, z, c: (x, y, z ^ 2, c))
Y_ONE = pairs(lambda x, y, z, c: (x, y ^ 1, z, c))
Y_THREE = pairs(lambda x, y, z, c: (x, y ^ 3, z, c))
X_ONE = pairs(lambda x, y, z, c: (x ^ 1, y, z, c))
X_TWO = pairs(lambda x, y, z, c: (x ^ 2, y, z, c))
X_THREE = pairs(lambda x, y, z, c: (x ^ 3, y, z, c))
WITH_Y = [pairs(lambda x, y, z, c, k=k: (x, y ^ k, z, c)) for k in (1, 2, 3)]
ALONG_Z = [
    [place(x, y, z, c) for z in range(Z_LO * Z_HI)]
    for x in range(X)
    for y in range(Y)
    for c in range(CORE)
]


def exchange(pieces, axis, groups):
    return lax.all_to_all(pieces, axis, 0, 0, tiled=True, axis_index_groups=groups)


def sent(x, moves):
    return lax.ppermute(x, BOTH, moves)


def after(x, *others):
    return lax.optimization_barrier((x, *others))[0]


def joined(x, came, *behind):
    return jnp.stack(lax.optimization_barrier((x, came, *behind))[:2])


def added(pieces):
    return pieces.astype(F32).sum(axis=0)


def dot(a, b, dims=((1,), (0,))):
    return lax.dot_general(a, b, (dims, ((), ())), preferred_element_type=F32)


COST = {'prepare_kernel': 1, 'gram_kernel': 3000, 'merge_kernel': 100, 'back_kernel': 2000, 'sum_kernel': 100, 'root_kernel': 0, 'region_kernel': 1500, 'root_rows_kernel': 30}
VMEM, SMEM, HBM = pltpu.VMEM, pltpu.SMEM, pltpu.HBM


def call(kernel, ins, outs, scratch, flops, mib, *args):
    flops = COST[kernel.func.__name__ if isinstance(kernel, functools.partial) else kernel.__name__]
    moved = 2 * sum(a.size for a in args) + 2 * sum(math.prod(s.shape) for s, _ in outs)
    args = [pltpu.with_memory_space_constraint(a, m) for a, m in zip(args, ins)]
    return pl.pallas_call(
        kernel,
        out_shape=[s if s.dtype == F32 else m(s.shape, s.dtype) for s, m in outs],
        in_specs=[pl.BlockSpec(memory_space=m) for m in ins],
        out_specs=[pl.BlockSpec(memory_space=m) for _, m in outs],
        scratch_shapes=scratch,
        compiler_params=pltpu.CompilerParams(vmem_limit_bytes=mib * 1024 * 1024),
        cost_estimate=pl.CostEstimate(flops=flops * 10**6, bytes_accessed=flops * 10**3, transcendentals=0),
    )(*args)


def position():
    r, leaf = lax.axis_index("region"), lax.axis_index("leaf")
    x, hi = lax.div(r, Z_HI), lax.rem(r, Z_HI)
    lo, rest = lax.div(leaf, Y * CORE), lax.rem(leaf, Y * CORE)
    return x, lax.div(rest, CORE), hi, lo, lax.rem(rest, CORE)


def shaped(*shape, dtype=BF):
    return jax.ShapeDtypeStruct(shape, dtype)


def dma(n):
    return pltpu.SemaphoreType.DMA((n,))


def prepare_kernel(root_f, root_a, region_f, region_a, root_out, region_out, sem):
    core = position()[4]
    copies = [
        pltpu.make_async_copy(region_f.at[0], region_out.at[0], sem.at[0]),
        pltpu.make_async_copy(region_a.at[0], region_out.at[1], sem.at[1]),
    ]
    for copy in copies:
        copy.start()

    @pl.when(core == 0)
    def _():
        copy = pltpu.make_async_copy(root_f, root_out, sem.at[2])
        copy.start()
        copy.wait()

    @pl.when(core != 0)
    def _():
        copy = pltpu.make_async_copy(root_a, root_out, sem.at[2])
        copy.start()
        copy.wait()

    for copy in copies:
        copy.wait()


def gram_kernel(
    w_hbm, root_hbm, region_hbm, white_hbm, own_ref, send_ref, w, leaf, white, in_sem, out_sem
):
    n, width = root_hbm.shape
    tiles = n // TILE
    first = position()[4] == 0
    arrivals, leaving = [], []
    for i in range(tiles):
        rows, k = pl.ds(TILE * i, TILE), pl.ds(0, TILE * (i + 1))
        arrivals.append(
            [
                pltpu.make_async_copy(w_hbm.at[rows, k], w.at[rows, k], in_sem.at[3 * i]),
                pltpu.make_async_copy(
                    root_hbm.at[rows], leaf.at[rows, pl.ds(0, width)], in_sem.at[3 * i + 1]
                ),
                pltpu.make_async_copy(
                    region_hbm.at[rows], leaf.at[rows, pl.ds(width, width)], in_sem.at[3 * i + 2]
                ),
            ]
        )
        for copy in arrivals[-1]:
            copy.start()
    for i in range(tiles):
        for copy in arrivals[i]:
            copy.wait()
        rows, k = slice(TILE * i, TILE * (i + 1)), TILE * (i + 1)
        for level in range(2):
            cols = slice(level * width, (level + 1) * width)
            white[rows, cols] = dot(w[rows, :k], leaf[:k, cols]).astype(BF)
        rows = pl.ds(TILE * i, TILE)
        leaving.append(
            pltpu.make_async_copy(white.at[rows], white_hbm.at[rows], out_sem.at[i])
        )
        leaving[-1].start()
    for level in range(2):
        a = white[:, level * width : (level + 1) * width]
        for i in range(width // TILE):
            g = dot(a[:, TILE * i : TILE * (i + 1)], a, ((0,), (0,)))
            g = g.reshape(TILE // 32, 2, 16, width)
            for b in range(TILE // 32):
                lo, y = divmod(i * (TILE // 32) + b, Y)
                own_ref[y, level, lo] = jnp.where(first, g[b, 0], g[b, 1]).astype(BF)
                send_ref[y, level, lo] = jnp.where(first, g[b, 1], g[b, 0]).astype(BF)
    for copy in leaving:
        copy.wait()


def back_kernel(w_hbm, white_hbm, out_hbm, w, white, out, in_sem, out_sem):
    n = w_hbm.shape[0]
    width = white.shape[1] // 2
    tiles = n // TILE
    arrivals, leaving = [], []
    for i in reversed(range(tiles)):
        rows, k = pl.ds(TILE * i, TILE), pl.ds(0, TILE * (i + 1))
        pair = [
            pltpu.make_async_copy(w_hbm.at[rows, k], w.at[rows, k], in_sem.at[2 * i]),
            pltpu.make_async_copy(white_hbm.at[rows], white.at[rows], in_sem.at[2 * i + 1]),
        ]
        for copy in pair:
            copy.start()
        arrivals.append(pair)
    for i, pair in zip(reversed(range(tiles)), arrivals):
        for copy in pair:
            copy.wait()
        rows = slice(TILE * i, TILE * (i + 1))
        for level in range(2):
            cols = slice(level * width, (level + 1) * width)
            out[rows, cols] = dot(
                w[TILE * i :, rows], white[TILE * i :, cols], ((0,), (0,))
            ).astype(BF)
        rows = pl.ds(TILE * i, TILE)
        leaving.append(pltpu.make_async_copy(out.at[rows], out_hbm.at[rows], out_sem.at[i]))
        leaving[-1].start()
    for copy in leaving:
        copy.wait()


def merge_kernel(own, came, *outs):
    y = position()[1]
    for k, out in enumerate(outs):
        out[...] = (own[y ^ k].astype(F32) + came[y ^ k].astype(F32)).astype(BF)


def sum_kernel(a, b, c, d, out):
    for level in range(2):
        for lo in range(Z_LO):
            total = a[level, lo].astype(F32) + b[level, lo].astype(F32)
            total = total + (c[level, lo].astype(F32) + d[level, lo].astype(F32))
            total = total.astype(BF)
            for hi in range(Z_HI):
                out[hi * Z_LO + lo, level] = total


def product_of_rows(total, factor, scale):
    high = total.astype(BF)
    low = (total - high.astype(F32)).astype(BF)
    out = dot(jnp.concatenate([high, low]), factor)
    return (out[:16] + out[16:]) * scale


def start_back(level, back_hbm, back, in_sem):
    width = back.shape[1]
    copies = []
    for i in range(back.shape[0] // TILE):
        rows = pl.ds(TILE * i, TILE)
        source = back_hbm.at[rows, pl.ds(level * width, width)]
        copies.append(pltpu.make_async_copy(source, back.at[rows], in_sem.at[i]))
        copies[-1].start()
    return copies


def gradients(arrivals, back, product, part, out, out_sem):
    leaving = []
    for i, copy in enumerate(arrivals):
        copy.wait()
        rows = pl.ds(TILE * i, TILE)
        part[rows, :] = dot(back[rows, :], product[...]).astype(BF)
        leaving.append(pltpu.make_async_copy(part.at[rows], out.at[0, rows], out_sem.at[i]))
        leaving[-1].start()
    for copy in leaving:
        copy.wait()


def factor_product(f, a):
    product = dot(f[...], a[...]) + dot(f[...], a[...], ((1,), (1,)))
    return product.astype(BF)


def root_kernel(mine_ref, came_ref, back_hbm, out_hbm, product, f, a, back, part, in_sem, out_sem):
    x, _, hi, _, core = position()
    first = core == 0
    arrivals = start_back(0, back_hbm, back, in_sem)
    for j in range(X * Z_HI):
        rows = slice(64 * j, 64 * (j + 1))
        v = x ^ (j // Z_HI)
        t = v >> 1
        slot = t * 4 + ((v & 1) ^ t) * 2 + (hi ^ (j % Z_HI))
        mine, came = mine_ref[slot], came_ref[slot]
        f[rows, :] = jnp.where(first, mine, came)
        a[rows, :] = jnp.where(first, came, mine)
    product[...] = factor_product(f, a)
    gradients(arrivals, back, product, part, out_hbm, out_sem)


def region_kernel(
    scale,
    mine_ref,
    came_ref,
    pieces,
    back_hbm,
    out_hbm,
    rows_out,
    f,
    a,
    product,
    back,
    part,
    in_sem,
    out_sem,
):
    _, y, hi, lo, core = position()
    first = core == 0
    arrivals = start_back(1, back_hbm, back, in_sem)
    for j in range(Z_LO * Y):
        v = y ^ (j % Y)
        t = v >> 1
        slot = t * 8 + ((v & 1) ^ t) * 4 + (lo ^ (j // Y))
        for k, out in ((0, f), (1, a)):
            mine, came = mine_ref[slot, k], came_ref[slot, k]
            out[32 * j : 32 * j + 16, :] = jnp.where(first, mine, came)
            out[32 * j + 16 : 32 * j + 32, :] = jnp.where(first, came, mine)
    product[...] = factor_product(f, a)
    total = pieces[hi * Z_LO, 1].astype(F32)
    for k in range(1, Z_LO):
        total = total + pieces[hi * Z_LO + k, 1].astype(F32)
    rows_out[0] = product_of_rows(total, product[...], scale)
    gradients(arrivals, back, product, part, out_hbm, out_sem)


def root_rows_kernel(scale, a, b, c, d, factor, out_ref):
    total = (a[...].astype(F32) + b[...].astype(F32)) + (c[...].astype(F32) + d[...].astype(F32))
    out_ref[...] = product_of_rows(total, factor[...], scale)


def on_device(
    whiten, leaf_root, leaf_region, root_factor, root_adjoint, region_factor, region_adjoint
):
    obs, width = leaf_root.shape[1:]
    tiles = obs // TILE
    w = whiten[0]

    root_mine, region_mine = call(
        prepare_kernel,
        [HBM] * 4,
        [(shaped(64, width), VMEM), (shaped(2, 16, width), VMEM)],
        [dma(3)],
        0,
        4,
        root_factor,
        root_adjoint,
        region_factor,
        region_adjoint,
    )
    w_first = after(w, root_mine)
    root_other, region_other = sent(root_mine, MIRROR_Z), sent(region_mine, Z_ONE)

    square, strip = VMEM((obs, 2 * width), BF), VMEM((obs, width), BF)
    half = shaped(Y, 2, Z_LO, 16, width)
    white, own, send = call(
        gram_kernel,
        [HBM] * 3,
        [(shaped(obs, 2 * width), HBM), (half, VMEM), (half, VMEM)],
        [VMEM((obs, obs), BF), square, square, dma(3 * tiles), dma(tiles)],
        2 * 2 * (obs * obs * width + obs * width * width),
        20,
        w_first,
        leaf_root[0],
        leaf_region[0],
    )
    send = after(send, root_other, region_other)
    quarter = shaped(2, Z_LO, 16, width)
    total, *shares = call(
        merge_kernel, [VMEM] * 2, [(quarter, VMEM)] * Y, [], 0, 8, own, sent(send, SWAP_CORES)
    )
    shares = [sent(shares[k], WITH_Y[k]) for k in (1, 0, 2)]
    root_mine = joined(root_mine, root_other)
    root_other = sent(root_mine, X_ONE)
    region_mine = joined(region_mine, region_other, send)
    region_other = sent(region_mine, Z_TWO)
    (back,) = call(
        back_kernel,
        [HBM] * 2,
        [(shaped(obs, 2 * width), HBM)],
        [VMEM((obs, obs), BF), square, square, dma(2 * tiles), dma(tiles)],
        2 * 2 * obs * obs * width,
        20,
        w,
        after(white, total),
    )
    root_mine = joined(root_mine, root_other, back)
    root_other = sent(root_mine, X_THREE)
    region_mine = joined(region_mine, region_other, total)
    region_other = sent(region_mine, Y_ONE)
    (leaf_total,) = call(
        sum_kernel,
        [VMEM] * Y,
        [(shaped(Z_LO * Z_HI, 2, 16, width), VMEM)],
        [],
        0,
        8,
        total,
        *shares,
    )
    root_mine = joined(root_mine, root_other, leaf_total).reshape(X * Z_HI, 64, width)
    root_came = sent(root_mine, SWAP_CORES)
    region_mine = joined(region_mine, region_other, leaf_total)
    region_other = sent(region_mine, Y_THREE)
    pieces = exchange(leaf_total, BOTH, ALONG_Z)
    scale = 1.0 / obs
    factor = VMEM((width, width), BF)
    held = [strip, strip, dma(tiles), dma(tiles)]
    work = 2 * obs * width * width + 4 * width**3
    grad_root, root_product = call(
        root_kernel,
        [VMEM] * 2 + [HBM],
        [(shaped(1, obs, width), HBM), (shaped(width, width), VMEM)],
        [factor, factor, *held],
        work,
        16,
        root_mine,
        root_came,
        back,
    )
    root_rows = added(after(pieces, root_product)[:, 0]).astype(BF)
    region_mine = joined(region_mine, region_other).reshape(Y * Z_LO, 2, 16, width)
    region_came = sent(region_mine, SWAP_CORES)
    others = [sent(root_rows, moves) for moves in (X_ONE, X_THREE, X_TWO)]

    grad_region, region_part = call(
        functools.partial(region_kernel, scale),
        [VMEM] * 3 + [HBM],
        [(shaped(1, obs, width), HBM), (shaped(1, 16, width, dtype=F32), VMEM)],
        [factor, factor, factor, *held],
        work,
        16,
        after(region_mine),
        region_came,
        pieces,
        back,
    )
    (root_part,) = call(
        functools.partial(root_rows_kernel, scale),
        [VMEM] * 5,
        [(shaped(16, width, dtype=F32), VMEM)],
        [],
        4 * 16 * width * width,
        4,
        after(root_rows, region_part),
        *others,
        root_product,
    )
    return grad_root, grad_region, root_part, region_part


def solution(mesh):
    return jax.shard_map(
        on_device,
        mesh=mesh,
        in_specs=(
            P(("region", "leaf"), None, None),
            P(("region", "leaf"), None, None),
            P(("region", "leaf"), None, None),
            P("region", None),
            P("region", None),
            P("region", "leaf", None),
            P("region", "leaf", None),
        ),
        out_specs=(
            P(("region", "leaf"), None, None),
            P(("region", "leaf"), None, None),
            P("leaf", None),
            P("region", "leaf", None),
        ),
        check_vma=False,
    )
```

```python
import functools
import math

import jax
import jax.numpy as jnp
from jax import lax
from jax.experimental import pallas as pl
from jax.experimental.pallas import tpu as pltpu
from jax.sharding import PartitionSpec as P

BF = jnp.bfloat16
F32 = jnp.float32
BOTH = ("region", "leaf")
Z_LO, Y, CORE, X, Z_HI = 4, 4, 2, 4, 2
LEAF = Z_LO * Y * CORE
TILE = 256


def place(x, y, z, c):
    return (x * Z_HI + z // Z_LO) * LEAF + (z % Z_LO) * Y * CORE + y * CORE + c


def coordinates(i):
    r, leaf = divmod(i, LEAF)
    x, hi = divmod(r, Z_HI)
    lo, rest = divmod(leaf, Y * CORE)
    y, c = divmod(rest, CORE)
    return x, y, hi * Z_LO + lo, c


def pairs(move):
    return [(i, place(*move(*coordinates(i)))) for i in range(X * Z_HI * LEAF)]


SWAP_CORES = pairs(lambda x, y, z, c: (x, y, z, 1 - c))
MIRROR_Z = pairs(lambda x, y, z, c: (x, y, 7 - z, c))
Z_ONE = pairs(lambda x, y, z, c: (x, y, z ^ 1, c))
Z_TWO = pairs(lambda x, y, z, c: (x, y, z ^ 2, c))
Y_ONE = pairs(lambda x, y, z, c: (x, y ^ 1, z, c))
Y_THREE = pairs(lambda x, y, z, c: (x, y ^ 3, z, c))
X_ONE = pairs(lambda x, y, z, c: (x ^ 1, y, z, c))
X_TWO = pairs(lambda x, y, z, c: (x ^ 2, y, z, c))
X_THREE = pairs(lambda x, y, z, c: (x ^ 3, y, z, c))
WITH_Y = [pairs(lambda x, y, z, c, k=k: (x, y ^ k, z, c)) for k in (1, 2, 3)]
ALONG_Z = [
    [place(x, y, z, c) for z in range(Z_LO * Z_HI)]
    for x in range(X)
    for y in range(Y)
    for c in range(CORE)
]


def exchange(pieces, axis, groups):
    return lax.all_to_all(pieces, axis, 0, 0, tiled=True, axis_index_groups=groups)


def sent(x, moves):
    return lax.ppermute(x, BOTH, moves)


def after(x, *others):
    return lax.optimization_barrier((x, *others))[0]


def joined(x, came, *behind):
    return jnp.stack(lax.optimization_barrier((x, came, *behind))[:2])


def added(pieces):
    return pieces.astype(F32).sum(axis=0)


def dot(a, b, dims=((1,), (0,))):
    return lax.dot_general(a, b, (dims, ((), ())), preferred_element_type=F32)


COST = {'prepare_kernel': 1, 'gram_kernel': 3000, 'merge_kernel': 100, 'back_kernel': 2000, 'sum_kernel': 100, 'root_kernel': 0, 'region_kernel': 1500, 'root_rows_kernel': 30}
VMEM, SMEM, HBM = pltpu.VMEM, pltpu.SMEM, pltpu.HBM


def call(kernel, ins, outs, scratch, flops, mib, *args):
    flops = COST[kernel.func.__name__ if isinstance(kernel, functools.partial) else kernel.__name__]
    moved = 2 * sum(a.size for a in args) + 2 * sum(math.prod(s.shape) for s, _ in outs)
    args = [pltpu.with_memory_space_constraint(a, m) for a, m in zip(args, ins)]
    return pl.pallas_call(
        kernel,
        out_shape=[s if s.dtype == F32 else m(s.shape, s.dtype) for s, m in outs],
        in_specs=[pl.BlockSpec(memory_space=m) for m in ins],
        out_specs=[pl.BlockSpec(memory_space=m) for _, m in outs],
        scratch_shapes=scratch,
        compiler_params=pltpu.CompilerParams(vmem_limit_bytes=mib * 1024 * 1024),
        cost_estimate=pl.CostEstimate(flops=flops * 10**6, bytes_accessed=flops * 10**3, transcendentals=0),
    )(*args)


def position():
    r, leaf = lax.axis_index("region"), lax.axis_index("leaf")
    x, hi = lax.div(r, Z_HI), lax.rem(r, Z_HI)
    lo, rest = lax.div(leaf, Y * CORE), lax.rem(leaf, Y * CORE)
    return x, lax.div(rest, CORE), hi, lo, lax.rem(rest, CORE)


def shaped(*shape, dtype=BF):
    return jax.ShapeDtypeStruct(shape, dtype)


def dma(n):
    return pltpu.SemaphoreType.DMA((n,))


def prepare_kernel(root_f, root_a, region_f, region_a, root_out, region_out, sem):
    core = position()[4]
    copies = [
        pltpu.make_async_copy(region_f.at[0], region_out.at[0], sem.at[0]),
        pltpu.make_async_copy(region_a.at[0], region_out.at[1], sem.at[1]),
    ]
    for copy in copies:
        copy.start()

    @pl.when(core == 0)
    def _():
        copy = pltpu.make_async_copy(root_f, root_out, sem.at[2])
        copy.start()
        copy.wait()

    @pl.when(core != 0)
    def _():
        copy = pltpu.make_async_copy(root_a, root_out, sem.at[2])
        copy.start()
        copy.wait()

    for copy in copies:
        copy.wait()


def gram_kernel(
    w_hbm, root_hbm, region_hbm, white_hbm, own_ref, send_ref, w, leaf, white, in_sem, out_sem
):
    n, width = root_hbm.shape
    tiles = n // TILE
    first = position()[4] == 0
    arrivals, leaving = [], []
    for i in range(tiles):
        rows, k = pl.ds(TILE * i, TILE), pl.ds(0, TILE * (i + 1))
        arrivals.append(
            [
                pltpu.make_async_copy(w_hbm.at[rows, k], w.at[rows, k], in_sem.at[3 * i]),
                pltpu.make_async_copy(
                    root_hbm.at[rows], leaf.at[rows, pl.ds(0, width)], in_sem.at[3 * i + 1]
                ),
                pltpu.make_async_copy(
                    region_hbm.at[rows], leaf.at[rows, pl.ds(width, width)], in_sem.at[3 * i + 2]
                ),
            ]
        )
        for copy in arrivals[-1]:
            copy.start()
    for i in range(tiles):
        for copy in arrivals[i]:
            copy.wait()
        rows, k = slice(TILE * i, TILE * (i + 1)), TILE * (i + 1)
        for level in range(2):
            cols = slice(level * width, (level + 1) * width)
            white[rows, cols] = dot(w[rows, :k], leaf[:k, cols]).astype(BF)
        rows = pl.ds(TILE * i, TILE)
        leaving.append(
            pltpu.make_async_copy(white.at[rows], white_hbm.at[rows], out_sem.at[i])
        )
        leaving[-1].start()
    for level in range(2):
        a = white[:, level * width : (level + 1) * width]
        for i in range(width // TILE):
            g = dot(a[:, TILE * i : TILE * (i + 1)], a, ((0,), (0,)))
            g = g.reshape(TILE // 32, 2, 16, width)
            for b in range(TILE // 32):
                lo, y = divmod(i * (TILE // 32) + b, Y)
                own_ref[y, level, lo] = jnp.where(first, g[b, 0], g[b, 1]).astype(BF)
                send_ref[y, level, lo] = jnp.where(first, g[b, 1], g[b, 0]).astype(BF)
    for copy in leaving:
        copy.wait()


def back_kernel(w_hbm, white_hbm, out, w, white, in_sem):
    n = w_hbm.shape[0]
    tiles = n // TILE
    arrivals = []
    for i in reversed(range(tiles)):
        rows, k = pl.ds(TILE * i, TILE), pl.ds(0, TILE * (i + 1))
        pair = [
            pltpu.make_async_copy(w_hbm.at[rows, k], w.at[rows, k], in_sem.at[2 * i]),
            pltpu.make_async_copy(white_hbm.at[rows], white.at[rows], in_sem.at[2 * i + 1]),
        ]
        for copy in pair:
            copy.start()
        arrivals.append(pair)
    for i, pair in zip(reversed(range(tiles)), arrivals):
        for copy in pair:
            copy.wait()
        rows = slice(TILE * i, TILE * (i + 1))
        product = dot(w[TILE * i :, rows], white[TILE * i :, :], ((0,), (0,)))
        out[rows, :] = product.astype(BF)


def merge_kernel(own, came, *outs):
    y = position()[1]
    for k, out in enumerate(outs):
        out[...] = (own[y ^ k].astype(F32) + came[y ^ k].astype(F32)).astype(BF)


def sum_kernel(a, b, c, d, out):
    for level in range(2):
        for lo in range(Z_LO):
            total = a[level, lo].astype(F32) + b[level, lo].astype(F32)
            total = total + (c[level, lo].astype(F32) + d[level, lo].astype(F32))
            total = total.astype(BF)
            for hi in range(Z_HI):
                out[hi * Z_LO + lo, level] = total


def product_of_rows(total, factor, scale):
    high = total.astype(BF)
    low = (total - high.astype(F32)).astype(BF)
    out = dot(jnp.concatenate([high, low]), factor)
    return (out[:16] + out[16:]) * scale


def gradients(level, back, product, part, out, out_sem):
    width = part.shape[1]
    leaving = []
    for i in range(part.shape[0] // TILE):
        rows = pl.ds(TILE * i, TILE)
        cols = slice(level * width, (level + 1) * width)
        part[rows, :] = dot(back[rows, cols], product[...]).astype(BF)
        leaving.append(pltpu.make_async_copy(part.at[rows], out.at[0, rows], out_sem.at[i]))
        leaving[-1].start()
    for copy in leaving:
        copy.wait()


def factor_product(f, a):
    product = dot(f[...], a[...]) + dot(f[...], a[...], ((1,), (1,)))
    return product.astype(BF)


def root_kernel(mine_ref, came_ref, back, out_hbm, product, f, a, part, out_sem):
    x, _, hi, _, core = position()
    first = core == 0
    for j in range(X * Z_HI):
        rows = slice(64 * j, 64 * (j + 1))
        v = x ^ (j // Z_HI)
        t = v >> 1
        slot = t * 4 + ((v & 1) ^ t) * 2 + (hi ^ (j % Z_HI))
        mine, came = mine_ref[slot], came_ref[slot]
        f[rows, :] = jnp.where(first, mine, came)
        a[rows, :] = jnp.where(first, came, mine)
    product[...] = factor_product(f, a)
    gradients(0, back, product, part, out_hbm, out_sem)


def region_kernel(
    scale,
    mine_ref,
    came_ref,
    pieces,
    back,
    out_hbm,
    rows_out,
    f,
    a,
    product,
    part,
    out_sem,
):
    _, y, hi, lo, core = position()
    first = core == 0
    for j in range(Z_LO * Y):
        v = y ^ (j % Y)
        t = v >> 1
        slot = t * 8 + ((v & 1) ^ t) * 4 + (lo ^ (j // Y))
        for k, out in ((0, f), (1, a)):
            mine, came = mine_ref[slot, k], came_ref[slot, k]
            out[32 * j : 32 * j + 16, :] = jnp.where(first, mine, came)
            out[32 * j + 16 : 32 * j + 32, :] = jnp.where(first, came, mine)
    product[...] = factor_product(f, a)
    total = pieces[hi * Z_LO, 1].astype(F32)
    for k in range(1, Z_LO):
        total = total + pieces[hi * Z_LO + k, 1].astype(F32)
    rows_out[0] = product_of_rows(total, product[...], scale)
    gradients(1, back, product, part, out_hbm, out_sem)


def root_rows_kernel(scale, a, b, c, d, factor, out_ref):
    total = (a[...].astype(F32) + b[...].astype(F32)) + (c[...].astype(F32) + d[...].astype(F32))
    out_ref[...] = product_of_rows(total, factor[...], scale)


def on_device(
    whiten, leaf_root, leaf_region, root_factor, root_adjoint, region_factor, region_adjoint
):
    obs, width = leaf_root.shape[1:]
    tiles = obs // TILE
    w = whiten[0]

    root_mine, region_mine = call(
        prepare_kernel,
        [HBM] * 4,
        [(shaped(64, width), VMEM), (shaped(2, 16, width), VMEM)],
        [dma(3)],
        0,
        4,
        root_factor,
        root_adjoint,
        region_factor,
        region_adjoint,
    )
    w_first = after(w, root_mine)
    root_other, region_other = sent(root_mine, MIRROR_Z), sent(region_mine, Z_ONE)

    square, strip = VMEM((obs, 2 * width), BF), VMEM((obs, width), BF)
    half = shaped(Y, 2, Z_LO, 16, width)
    white, own, send = call(
        gram_kernel,
        [HBM] * 3,
        [(shaped(obs, 2 * width), HBM), (half, VMEM), (half, VMEM)],
        [VMEM((obs, obs), BF), square, square, dma(3 * tiles), dma(tiles)],
        2 * 2 * (obs * obs * width + obs * width * width),
        20,
        w_first,
        leaf_root[0],
        leaf_region[0],
    )
    send = after(send, root_other, region_other)
    quarter = shaped(2, Z_LO, 16, width)
    total, *shares = call(
        merge_kernel, [VMEM] * 2, [(quarter, VMEM)] * Y, [], 0, 8, own, sent(send, SWAP_CORES)
    )
    shares = [sent(shares[k], WITH_Y[k]) for k in (1, 0, 2)]
    root_mine = joined(root_mine, root_other)
    root_other = sent(root_mine, X_ONE)
    region_mine = joined(region_mine, region_other, send)
    region_other = sent(region_mine, Z_TWO)
    (back,) = call(
        back_kernel,
        [HBM] * 2,
        [(shaped(obs, 2 * width), VMEM)],
        [VMEM((obs, obs), BF), square, dma(2 * tiles)],
        2 * 2 * obs * obs * width,
        20,
        w,
        after(white, total),
    )
    root_mine = joined(root_mine, root_other, back)
    root_other = sent(root_mine, X_THREE)
    region_mine = joined(region_mine, region_other, total)
    region_other = sent(region_mine, Y_ONE)
    (leaf_total,) = call(
        sum_kernel,
        [VMEM] * Y,
        [(shaped(Z_LO * Z_HI, 2, 16, width), VMEM)],
        [],
        0,
        8,
        total,
        *shares,
    )
    root_mine = joined(root_mine, root_other, leaf_total).reshape(X * Z_HI, 64, width)
    root_came = sent(root_mine, SWAP_CORES)
    region_mine = joined(region_mine, region_other, leaf_total)
    region_other = sent(region_mine, Y_THREE)
    pieces = exchange(leaf_total, BOTH, ALONG_Z)
    scale = 1.0 / obs
    factor = VMEM((width, width), BF)
    held = [strip, dma(tiles)]
    work = 2 * obs * width * width + 4 * width**3
    grad_root, root_product = call(
        root_kernel,
        [VMEM] * 3,
        [(shaped(1, obs, width), HBM), (shaped(width, width), VMEM)],
        [factor, factor, *held],
        work,
        16,
        root_mine,
        root_came,
        back,
    )
    root_rows = added(after(pieces, root_product)[:, 0]).astype(BF)
    region_mine = joined(region_mine, region_other).reshape(Y * Z_LO, 2, 16, width)
    region_came = sent(region_mine, SWAP_CORES)
    others = [sent(root_rows, moves) for moves in (X_ONE, X_THREE, X_TWO)]

    grad_region, region_part = call(
        functools.partial(region_kernel, scale),
        [VMEM] * 4,
        [(shaped(1, obs, width), HBM), (shaped(1, 16, width, dtype=F32), VMEM)],
        [factor, factor, factor, *held],
        work,
        16,
        after(region_mine),
        region_came,
        pieces,
        back,
    )
    (root_part,) = call(
        functools.partial(root_rows_kernel, scale),
        [VMEM] * 5,
        [(shaped(16, width, dtype=F32), VMEM)],
        [],
        4 * 16 * width * width,
        4,
        after(root_rows, region_part),
        *others,
        root_product,
    )
    return grad_root, grad_region, root_part, region_part


def solution(mesh):
    return jax.shard_map(
        on_device,
        mesh=mesh,
        in_specs=(
            P(("region", "leaf"), None, None),
            P(("region", "leaf"), None, None),
            P(("region", "leaf"), None, None),
            P("region", None),
            P("region", None),
            P("region", "leaf", None),
            P("region", "leaf", None),
        ),
        out_specs=(
            P(("region", "leaf"), None, None),
            P(("region", "leaf"), None, None),
            P("leaf", None),
            P("region", "leaf", None),
        ),
        check_vma=False,
    )
```
